32 devices in a mesh: prow: 4 (over y, x), pcol: 8 (over z, core).
Axes of the slice: x: 2, y: 2, z: 4, core: 2. Of those that a mesh axis runs over, the one named last changes fastest.
Arguments:
- right_side: float32 [34, 8, 32768], P(None, 'pcol', 'prow'), may hold values from -6 to 6
- inverse_rows: float32 [34, 8, 512, 512], P(None, 'pcol', 'prow'), may hold values from -0.25 to 0.25
- panels: float32 [34, 8, 7, 512, 512], P(None, 'pcol', None, 'prow'), may hold values from -0.0625 to 0.0625
- pattern: int32 [34, 8, 7], P(None, 'pcol'), may hold values 0 or 1
- node_sizes: int32 [34, 8], P(None, 'pcol'), may hold values from 256 to 512
- parent: int32 [254], replicated, may hold values from 128 to 254, as said below
Outputs:
- solution: float32 [34, 8, 32768], P(None, 'pcol', 'prow')
The draws below stay inside these ranges and needn't reach their ends.
Inputs may be any that keep to these rules, and one draw needn't show every extreme that they name: Nodes are numbered level by level from the leaves (128 of them, halving up to one root); entry g is the number of node g's parent, which lies on the next level up, and every node above the leaves has exactly two children.
All inputs are finite; a program needn't handle non-finite values. No bound on the sum of `pattern` on one device may be relied on, other than what follows from the above.
Results may differ from the reference program's by a relative error of at most 0.0001.
Values sent between devices are 32-bit elements; how exact they have to be, the bound alone decides.
A program may use at most 128 MiB of HBM per device.

```python
import jax
import jax.numpy as jnp
from jax import lax

W = 512
R = 64
LEVELS = 8
LEAVES = 128
ANC = 7
SLOTS = 34
N_PCOL = 8


def draw_parent(key, part):
    pieces = []
    for height in range(LEVELS - 1):
        level_nodes = LEAVES >> height
        shuffled = jax.random.permutation(jax.random.fold_in(key, height + 11), level_nodes).astype(jnp.int32)
        upper_base = 2 * LEAVES - (LEAVES >> height)
        pieces.append(upper_base + shuffled // 2)
    return jnp.concatenate(pieces, 0).astype(jnp.int32)


def touch_ends(drawn, rng, least, high):
    longest = drawn.shape.index(max(drawn.shape))
    spots = []
    for shift in (0, 1):
        where = [jax.random.randint(jax.random.fold_in(rng, axis), (), 0, length) for axis, length in enumerate(drawn.shape)]
        where[longest] = (where[longest] + shift) % drawn.shape[longest]
        spots.append(tuple(where))
    return drawn.at[spots[0]].set(least).at[spots[1]].set(high)


def level_of(stream_key, dims, cuts, least, largest):
    loudness, own = 1.0, jax.random.fold_in(stream_key, 6)
    for position, shards_of in cuts:
        heights = jnp.exp(jax.random.uniform(jax.random.fold_in(own, position), (shards_of,), jnp.float32, least / len(cuts), largest / len(cuts)))
        loudness = loudness * jnp.repeat(heights, dims[position] // shards_of).reshape([-1 if axis == position else 1 for axis in range(len(dims))])
    return loudness


def scatter_about(key, dims, spread, limit, cuts=(), kind=jnp.bfloat16):
    loudness = level_of(key, dims, cuts, -0.22, 0.18) if cuts else 1.0
    values = jax.random.normal(key, dims, jnp.float32) * spread * loudness
    return jnp.minimum(jnp.maximum(values, -limit), limit).astype(kind)


def setup_inputs(seed: int = 0) -> dict:
    keys = jax.random.split(jax.random.key(seed), 7)
    right_side = scatter_about(keys[0], (SLOTS, N_PCOL, W * R), 1.0, 6.0, ((1, 8), (2, 4)), jnp.float32)
    inverse_rows = scatter_about(keys[1], (SLOTS, N_PCOL, W, W), W ** -0.5, 0.25, ((1, 8), (2, 4)), jnp.float32)
    panels = scatter_about(keys[2], (SLOTS, N_PCOL, ANC, W, W), (W * 16) ** -0.5, 0.0625, ((1, 8), (3, 4)), jnp.float32)
    pattern = touch_ends((jax.random.randint(keys[3], (SLOTS, N_PCOL, ANC), 0, 2) < 1).astype(jnp.int32), jax.random.fold_in(keys[3], 1), 0, 1)
    node_sizes = touch_ends(jax.random.randint(keys[4], (SLOTS, N_PCOL), W // 2, W + 1), jax.random.fold_in(keys[4], 1), W // 2, W).astype(jnp.int32)
    parent = draw_parent(jax.random.fold_in(keys[6], 71), 0)
    return dict(right_side=right_side, inverse_rows=inverse_rows, panels=panels, pattern=pattern, node_sizes=node_sizes, parent=parent)


def level_offset(height):
    return 2 * LEAVES - 2 * (LEAVES >> height)


def reference(right_side, inverse_rows, panels, pattern, node_sizes, parent):
    col_count = N_PCOL
    solution = jnp.zeros_like(right_side)
    updates = {}
    for height in range(1, LEVELS):
        updates[height] = jnp.zeros((LEAVES >> height, W, R), jnp.float32)
    slot_base = 0
    for height in range(LEVELS):
        level_nodes = LEAVES >> height
        node_index = jnp.arange(level_nodes, dtype=jnp.int32)
        slot_index = slot_base + node_index // col_count
        col_index = node_index % col_count
        residue = right_side[slot_index, col_index].reshape(level_nodes, W, R)
        if height > 0:
            residue = residue - updates[height]
        live_rows = (jnp.arange(W, dtype=jnp.int32)[None, :] < node_sizes[slot_index, col_index][:, None]).astype(jnp.float32)
        residue = residue * live_rows[:, :, None]
        inverse = inverse_rows[slot_index, col_index]
        solved = jnp.einsum("nvw,nvq->nwq", inverse, residue, precision=lax.Precision.HIGHEST)
        solved = solved * live_rows[:, :, None]
        solution = solution.at[slot_index, col_index].set(solved.reshape(level_nodes, W * R))
        ancestor = level_offset(height) + node_index
        for distance in range(LEVELS - 1 - height):
            ancestor = parent[ancestor]
            target = height + 1 + distance
            block = panels[slot_index, col_index, distance]
            contrib = jnp.einsum("nwv,nvq->nwq", block, solved, precision=lax.Precision.HIGHEST)
            contrib = contrib * pattern[slot_index, col_index, distance].astype(jnp.float32)[:, None, None]
            onehot = ((ancestor - level_offset(target))[:, None] == jnp.arange(LEAVES >> target, dtype=jnp.int32)[None, :]).astype(jnp.float32)
            updates[target] = updates[target] + jnp.einsum("nt,nwq->twq", onehot, contrib, precision=lax.Precision.HIGHEST)
        slot_base = slot_base + max(1, level_nodes // col_count)
    return solution
```

```python
import functools

import jax
import jax.numpy as jnp
from jax import lax
from jax.experimental import pallas as pl
from jax.experimental.pallas import tpu as pltpu
from jax.sharding import PartitionSpec as P

LEVELS = 8
LEAVES = 128
GROUP = 4
RING = 12
MESH = pl.DeviceIdType.MESH


class Plan:
    def __init__(self, rows, cols):
        self.rows, self.cols = rows, cols
        self.depth = cols // 2
        self.nodes = [LEAVES >> h for h in range(LEVELS)]
        self.slots = [max(1, n // cols) for n in self.nodes]
        self.slot_base, self.node_base, self.pend_base = [], [], []
        self.half_base, self.far_base = [], []
        s = n = p = c = f = 0
        for h in range(LEVELS):
            self.slot_base.append(s)
            self.node_base.append(n)
            self.pend_base.append(p)
            self.half_base.append(c)
            self.far_base.append(f)
            s += self.slots[h]
            n += self.nodes[h]
            if h > 0:
                p += self.slots[h] * cols
                c += self.slots[h] * self.depth
                f += self.slots[h] * (self.depth - 1)
        self.total, self.pend, self.half, self.far = s, p, c, f
        self.groups = []
        for h in range(LEVELS):
            size = min(GROUP, self.slots[h])
            for start in range(0, self.slots[h], size):
                self.groups.append((h, self.slot_base[h] + start, size))
        self.level_of = [h for h in range(LEVELS) for _ in range(self.slots[h])]


def split_pair(packed, low_lanes):
    high = packed.astype(jnp.bfloat16).astype(jnp.float32)
    low = packed - high
    top = jnp.where(low_lanes, high, pltpu.roll(low, 64, 1))
    bottom = jnp.where(low_lanes, pltpu.roll(high, 64, 1), low)
    return jnp.concatenate([top, bottom], 0).astype(jnp.bfloat16)


def two_part(matrix):
    high = matrix.astype(jnp.bfloat16)
    low = (matrix - high.astype(jnp.float32)).astype(jnp.bfloat16)
    return high, low


def kernel(
    plan, parent, pattern, sizes, rhs, inverse_hbm, panels_hbm, out,
    inverse, ring, pend, near, far, parts, arrived, solved, wide, blocks,
    target, weight, live,
    inverse_sem, ring_sem, near_sem, far_send, far_recv, part_send, part_recv, sol_send, sol_recv,
):
    rows, cols, depth = plan.rows, plan.cols, plan.depth
    piece = inverse.shape[1]
    half = piece // 2
    my_row, my_col = lax.axis_index("prow"), lax.axis_index("pcol")
    my_core, my_z = lax.rem(my_col, 2), lax.div(my_col, 2)
    row_peers = [lax.rem(my_row + d, rows) for d in range(1, rows)]
    z_peers = [lax.rem(my_z + d, depth) for d in range(1, depth)]
    mate = my_col + 1 - 2 * my_core

    loads = []
    for h in range(LEVELS):
        span = pl.ds(plan.slot_base[h], plan.slots[h])
        copy = pltpu.make_async_copy(inverse_hbm.at[span], inverse.at[span], inverse_sem.at[h])
        copy.start()
        loads.append(copy)
    panel_loads = {}

    def load_panel(slot):
        if slot >= plan.total:
            return
        reach = LEVELS - 1 - plan.level_of[slot]
        if reach == 0:
            return
        place = slot % RING
        copy = pltpu.make_async_copy(
            panels_hbm.at[slot, pl.ds(0, reach)], ring.at[place, pl.ds(0, reach)], ring_sem.at[place]
        )
        copy.start()
        panel_loads[slot] = copy

    for slot in range(min(RING, plan.total)):
        load_panel(slot)

    barrier = pltpu.get_barrier_semaphore()
    greeted = [(p, my_col) for p in row_peers] + [(my_row, mate)]
    greeted += [(my_row, z * 2 + my_core) for z in z_peers]
    for who in greeted:
        pl.semaphore_signal(barrier, inc=1, device_id=who, device_id_type=MESH)

    for h in range(LEVELS):

        def describe(i, carry, h=h):
            slot = plan.slot_base[h] + i
            place = i * cols + my_col
            real = place < plan.nodes[h]
            live[slot] = jnp.where(real, sizes[slot], 0)
            node = plan.node_base[h] + jnp.minimum(place, plan.nodes[h] - 1)
            for a in range(LEVELS - 1 - h):
                up = h + 1 + a
                node = parent[node]
                local = node - plan.node_base[up]
                owner = lax.rem(local, cols)
                spot = lax.rem(owner, 2) * depth + lax.div(owner, 2)
                target[slot * 7 + a] = spot * plan.slots[up] + lax.div(local, cols)
                weight[slot * 7 + a] = jnp.where(real, pattern[slot * 7 + a], 0).astype(jnp.float32)
            return carry

        lax.fori_loop(0, plan.slots[h], describe, 0)

    def clear(i, carry):
        pend[i] = jnp.zeros_like(pend[i])
        return carry

    lax.fori_loop(0, plan.pend, clear, 0)

    lane = lax.broadcasted_iota(jnp.int32, (half, 128), 1)
    low_lanes = lane < 64
    row_ids = (
        my_row * piece
        + lax.broadcasted_iota(jnp.int32, (half, 128), 0)
        + jnp.where(low_lanes, 0, half)
    )
    contract_first = (((0,), (0,)), ((), ()))
    sends = []

    pl.semaphore_wait(barrier, len(greeted))

    def remote(src, dst, send_sem, recv_sem, who):
        copy = pltpu.make_async_remote_copy(
            src_ref=src, dst_ref=dst, send_sem=send_sem, recv_sem=recv_sem,
            device_id=who, device_id_type=MESH,
        )
        copy.start()
        sends.append(copy)
        return copy

    def start_partial(g):
        h, base, size = plan.groups[g]

        def body(n, carry):
            slot = base + n
            residue = rhs[slot]
            if h > 0:
                step = slot - plan.slot_base[h]
                own = (my_core * depth + my_z) * plan.slots[h] + step
                update = pend[plan.pend_base[h] + own]
                for d in range(depth - 1):
                    update = update + far[plan.far_base[h] + d * plan.slots[h] + step]
                residue = residue - update
            scaled = jnp.where(row_ids < live[slot], residue, 0.0)
            pair = split_pair(scaled, low_lanes)
            high, low = two_part(inverse[slot])
            both = lax.dot_general(high, pair, contract_first, preferred_element_type=jnp.float32)
            both += lax.dot_general(low, pair, contract_first, preferred_element_type=jnp.float32)
            both += pltpu.roll(both, 64, 1)
            for r in range(rows):
                first = both[r * piece : r * piece + half]
                second = both[r * piece + half : (r + 1) * piece]
                parts[r, slot] = jnp.where(low_lanes, first, second)
            return carry

        lax.fori_loop(0, size, body, 0)
        span = pl.ds(base, size)
        return [
            remote(
                parts.at[peer, span], arrived.at[d, span],
                part_send.at[g, d], part_recv.at[g, d], (peer, my_col),
            )
            for d, peer in enumerate(row_peers)
        ]

    def start_solved(g, copies):
        h, base, size = plan.groups[g]
        for copy in copies:
            copy.wait_recv()

        def body(n, carry):
            slot = base + n
            total = parts[my_row, slot]
            for d in range(rows - 1):
                total = total + arrived[d, slot]
            total = jnp.where(row_ids < live[slot], total, 0.0)
            solved[my_row, slot] = total
            out[slot] = total
            return carry

        lax.fori_loop(0, size, body, 0)
        if h == LEVELS - 1:
            return []
        span = pl.ds(base, size)
        return [
            remote(
                solved.at[my_row, span], solved.at[my_row, span],
                sol_send.at[g, d], sol_recv.at[g, d], (peer, my_col),
            )
            for d, peer in enumerate(row_peers)
        ]

    def widen(g, copies):
        h, base, size = plan.groups[g]
        for copy in copies:
            copy.wait_recv()

        def body(n, carry):
            for r in range(rows):
                wide[n, pl.ds(r * piece, piece)] = split_pair(solved[r, base + n], low_lanes)
            return carry

        lax.fori_loop(0, size, body, 0)
        for slot in range(base, base + size):
            panel_loads[slot].wait()

    def contribute(g, first, last):
        h, base, size = plan.groups[g]
        if first >= last:
            return

        def body(n, carry):
            place = lax.rem(base + n, RING)
            pair = wide[n]
            for a in range(first, last):
                high, low = two_part(ring[place, a])
                both = jnp.dot(high, pair, preferred_element_type=jnp.float32)
                both += jnp.dot(low, pair, preferred_element_type=jnp.float32)
                both += pltpu.roll(both, 64, 1)
                blocks[n, a] = jnp.where(low_lanes, both[:half], both[half:])
            return carry

        lax.fori_loop(0, size, body, 0)
        for a in range(first, last):
            up = h + 1 + a
            goals = [target[(base + n) * 7 + a] for n in range(size)]
            scales = [weight[(base + n) * 7 + a] for n in range(size)]

            def scatter(t, carry, a=a, up=up, goals=goals, scales=scales):
                total = pend[plan.pend_base[up] + t]
                for n in range(size):
                    total = total + jnp.where(goals[n] == t, scales[n], 0.0) * blocks[n, a]
                pend[plan.pend_base[up] + t] = total
                return carry

            lax.fori_loop(0, plan.slots[up] * cols, scatter, 0)

    def start_near(h):
        count = plan.slots[h] * depth
        return remote(
            pend.at[pl.ds(plan.pend_base[h] + (1 - my_core) * count, count)],
            near.at[pl.ds(plan.half_base[h], count)],
            near_sem.at[0, h], near_sem.at[1, h], (my_row, mate),
        )

    def start_far(h, copy):
        count = plan.slots[h] * depth
        mine = plan.pend_base[h] + my_core * count
        copy.wait_recv()

        def body(i, carry):
            pend[mine + i] = pend[mine + i] + near[plan.half_base[h] + i]
            return carry

        lax.fori_loop(0, count, body, 0)
        return [
            remote(
                pend.at[pl.ds(mine + z * plan.slots[h], plan.slots[h])],
                far.at[pl.ds(plan.far_base[h] + d * plan.slots[h], plan.slots[h])],
                far_send.at[h, d], far_recv.at[h, d], (my_row, z * 2 + my_core),
            )
            for d, z in enumerate(z_peers)
        ]

    group_ids = {h: [g for g, one in enumerate(plan.groups) if one[0] == h] for h in range(LEVELS)}
    for h in range(LEVELS):
        reach = LEVELS - 1 - h
        ids = group_ids[h]
        loads[h].wait()
        waiting = [start_partial(g) for g in ids]
        sharing = {ids[0]: start_solved(ids[0], waiting[0])}
        for i, g in enumerate(ids):
            if i + 1 < len(ids):
                sharing[ids[i + 1]] = start_solved(ids[i + 1], waiting[i + 1])
            if reach == 0:
                continue
            widen(g, sharing[g])
            final = i + 1 == len(ids)
            contribute(g, 0, 1)
            if final:
                near_copy = start_near(h + 1)
            contribute(g, 1, min(2, reach))
            if final:
                far_copies = start_far(h + 1, near_copy)
            contribute(g, 2, reach)
            _, base, size = plan.groups[g]
            for slot in range(base, base + size):
                load_panel(slot + RING)
            if final:
                for copy in far_copies:
                    copy.wait_recv()
    for copy in sends:
        copy.wait_send()


def on_device(right_side, inverse_rows, panels, pattern, node_sizes, parent):
    rows, cols = lax.axis_size("prow"), lax.axis_size("pcol")
    plan = Plan(rows, cols)
    slots, piece, full = plan.total, panels.shape[3], panels.shape[4]
    count = right_side.shape[2] // piece
    half = piece // 2
    packed = right_side.reshape(slots, 2, half, count).swapaxes(1, 2).reshape(slots, half, 2 * count)
    groups = len(plan.groups)
    dma = pltpu.SemaphoreType.DMA
    vmem = pl.BlockSpec(memory_space=pltpu.VMEM)
    smem = pl.BlockSpec(memory_space=pltpu.SMEM)
    anywhere = pl.BlockSpec(memory_space=pl.ANY)
    block = (half, 2 * count)
    solved = pl.pallas_call(
        functools.partial(kernel, plan),
        out_shape=jax.ShapeDtypeStruct((slots,) + block, jnp.float32),
        in_specs=[smem, smem, smem, vmem, anywhere, anywhere],
        out_specs=vmem,
        scratch_shapes=[
            pltpu.VMEM((slots, piece, full), jnp.float32),
            pltpu.VMEM((RING, LEVELS - 1, piece, full), jnp.float32),
            pltpu.VMEM((plan.pend,) + block, jnp.float32),
            pltpu.VMEM((plan.half,) + block, jnp.float32),
            pltpu.VMEM((plan.far,) + block, jnp.float32),
            pltpu.VMEM((rows, slots) + block, jnp.float32),
            pltpu.VMEM((rows - 1, slots) + block, jnp.float32),
            pltpu.VMEM((rows, slots) + block, jnp.float32),
            pltpu.VMEM((GROUP, full, 2 * count), jnp.bfloat16),
            pltpu.VMEM((GROUP, LEVELS - 1) + block, jnp.float32),
            pltpu.SMEM((slots * 7,), jnp.int32),
            pltpu.SMEM((slots * 7,), jnp.float32),
            pltpu.SMEM((slots,), jnp.int32),
            dma((LEVELS,)),
            dma((RING,)),
            dma((2, LEVELS)),
            dma((LEVELS, plan.depth - 1)),
            dma((LEVELS, plan.depth - 1)),
            dma((groups, rows - 1)),
            dma((groups, rows - 1)),
            dma((groups, rows - 1)),
            dma((groups, rows - 1)),
        ],
        compiler_params=pltpu.CompilerParams(
            collective_id=0, has_side_effects=True, vmem_limit_bytes=60 * 1024 * 1024
        ),
    )(
        parent,
        pattern.reshape(slots * 7),
        node_sizes.reshape(slots),
        packed,
        inverse_rows.reshape(slots, piece, full),
        panels.reshape(slots, LEVELS - 1, piece, full),
    )
    return solved.reshape(slots, half, 2, count).swapaxes(1, 2).reshape(slots, 1, piece * count)


def solution(mesh):
    in_specs = (
        P(None, "pcol", "prow"),
        P(None, "pcol", "prow", None),
        P(None, "pcol", None, "prow", None),
        P(None, "pcol", None),
        P(None, "pcol"),
        P(),
    )
    out_specs = P(None, "pcol", "prow")
    return jax.shard_map(
        on_device, mesh=mesh, in_specs=in_specs, out_specs=out_specs, check_vma=False
    )
```

```python
import functools

import jax
import jax.numpy as jnp
from jax import lax
from jax.experimental import pallas as pl
from jax.experimental.pallas import tpu as pltpu
from jax.sharding import PartitionSpec as P

LEVELS = 8
LEAVES = 128
GROUP = 4
RING = 12
MESH = pl.DeviceIdType.MESH


class Plan:
    def __init__(self, rows, cols):
        self.rows, self.cols = rows, cols
        self.depth = cols // 2
        self.nodes = [LEAVES >> h for h in range(LEVELS)]
        self.slots = [max(1, n // cols) for n in self.nodes]
        self.slot_base, self.node_base, self.pend_base = [], [], []
        self.half_base, self.far_base = [], []
        s = n = p = c = f = 0
        for h in range(LEVELS):
            self.slot_base.append(s)
            self.node_base.append(n)
            self.pend_base.append(p)
            self.half_base.append(c)
            self.far_base.append(f)
            s += self.slots[h]
            n += self.nodes[h]
            if h > 0:
                p += self.slots[h] * cols
                c += self.slots[h] * self.depth
                f += self.slots[h] * (self.depth - 1)
        self.total, self.pend, self.half, self.far = s, p, c, f
        self.groups = []
        for h in range(LEVELS):
            size = GROUP if h == 0 else min(2, max(1, self.slots[h] // 2))
            size = min(size, self.slots[h])
            for start in range(0, self.slots[h], size):
                self.groups.append((h, self.slot_base[h] + start, size))
        self.level_of = [h for h in range(LEVELS) for _ in range(self.slots[h])]


def split_pair(packed, low_lanes):
    high = packed.astype(jnp.bfloat16).astype(jnp.float32)
    low = packed - high
    top = jnp.where(low_lanes, high, pltpu.roll(low, 64, 1))
    bottom = jnp.where(low_lanes, pltpu.roll(high, 64, 1), low)
    return jnp.concatenate([top, bottom], 0).astype(jnp.bfloat16)


def two_part(matrix):
    high = matrix.astype(jnp.bfloat16)
    low = (matrix - high.astype(jnp.float32)).astype(jnp.bfloat16)
    return high, low


def kernel(
    plan, parent, pattern, sizes, rhs, inverse_hbm, panels_hbm, out,
    inverse, ring, pend, near, far, parts, arrived, solved, wide, blocks,
    target, weight, live, flip,
    inverse_sem, ring_sem, near_sem, far_send, far_recv, part_send, part_recv, sol_send, sol_recv,
):
    rows, cols, depth = plan.rows, plan.cols, plan.depth
    piece = inverse.shape[1]
    half = piece // 2
    my_row, my_col = lax.axis_index("prow"), lax.axis_index("pcol")
    my_core, my_z = lax.rem(my_col, 2), lax.div(my_col, 2)
    row_peers = [lax.rem(my_row + d, rows) for d in range(1, rows)]
    z_peers = [lax.rem(my_z + d, depth) for d in range(1, depth)]
    mate = my_col + 1 - 2 * my_core

    loads = []
    for h in range(LEVELS):
        span = pl.ds(plan.slot_base[h], plan.slots[h])
        copy = pltpu.make_async_copy(inverse_hbm.at[span], inverse.at[span], inverse_sem.at[h])
        copy.start()
        loads.append(copy)
    panel_loads = {}

    def load_panel(slot):
        if slot >= plan.total:
            return
        reach = LEVELS - 1 - plan.level_of[slot]
        if reach == 0:
            return
        place = slot % RING
        copy = pltpu.make_async_copy(
            panels_hbm.at[slot, pl.ds(0, reach)], ring.at[place, pl.ds(0, reach)], ring_sem.at[place]
        )
        copy.start()
        panel_loads[slot] = copy

    for slot in range(min(RING, plan.total)):
        load_panel(slot)

    barrier = pltpu.get_barrier_semaphore()
    greeted = [(p, my_col) for p in row_peers] + [(my_row, mate)]
    greeted += [(my_row, z * 2 + my_core) for z in z_peers]
    for who in greeted:
        pl.semaphore_signal(barrier, inc=1, device_id=who, device_id_type=MESH)

    for h in range(LEVELS):

        def describe(i, carry, h=h):
            slot = plan.slot_base[h] + i
            place = i * cols + my_col
            real = place < plan.nodes[h]
            live[slot] = jnp.where(real, sizes[slot, 0], 0)
            node = plan.node_base[h] + jnp.minimum(place, plan.nodes[h] - 1)
            for a in range(LEVELS - 1 - h):
                up = h + 1 + a
                node = parent[node]
                local = node - plan.node_base[up]
                owner = lax.rem(local, cols)
                spot = lax.rem(owner, 2) * depth + lax.div(owner, 2)
                target[slot * 7 + a] = spot * plan.slots[up] + lax.div(local, cols)
                weight[slot * 7 + a] = jnp.where(real, pattern[slot, 0, a], 0).astype(jnp.float32)
            return carry

        lax.fori_loop(0, plan.slots[h], describe, 0)

    def clear(i, carry):
        pend[i] = jnp.zeros_like(pend[i])
        return carry

    lax.fori_loop(0, plan.pend, clear, 0)

    lane = lax.broadcasted_iota(jnp.int32, (half, 128), 1)
    low_lanes = lane < 64
    row_ids = (
        my_row * piece
        + lax.broadcasted_iota(jnp.int32, (half, 128), 0)
        + jnp.where(low_lanes, 0, half)
    )
    contract_first = (((0,), (0,)), ((), ()))
    sends = []

    def pack_halves(slot, carry):
        pairs = rhs[slot]
        flip[pl.ds(0, half, stride=2)] = pairs
        flip[pl.ds(1, half, stride=2)] = pltpu.roll(pairs, 64, 1)
        out[slot] = jnp.where(low_lanes, flip[:half], pltpu.roll(flip[half:], 64, 1))
        return carry

    lax.fori_loop(0, plan.total, pack_halves, 0)

    pl.semaphore_wait(barrier, len(greeted))

    def remote(src, dst, send_sem, recv_sem, who):
        copy = pltpu.make_async_remote_copy(
            src_ref=src, dst_ref=dst, send_sem=send_sem, recv_sem=recv_sem,
            device_id=who, device_id_type=MESH,
        )
        copy.start()
        sends.append(copy)
        return copy

    def start_partial(g):
        h, base, size = plan.groups[g]

        def body(n, carry):
            slot = base + n
            residue = out[slot]
            if h > 0:
                step = slot - plan.slot_base[h]
                own = (my_core * depth + my_z) * plan.slots[h] + step
                update = pend[plan.pend_base[h] + own]
                for d in range(depth - 1):
                    update = update + far[plan.far_base[h] + d * plan.slots[h] + step]
                residue = residue - update
            scaled = jnp.where(row_ids < live[slot], residue, 0.0)
            pair = split_pair(scaled, low_lanes)
            high, low = two_part(inverse[slot])
            both = lax.dot_general(high, pair, contract_first, preferred_element_type=jnp.float32)
            both += lax.dot_general(low, pair, contract_first, preferred_element_type=jnp.float32)
            both += pltpu.roll(both, 64, 1)
            for r in range(rows):
                first = both[r * piece : r * piece + half]
                second = both[r * piece + half : (r + 1) * piece]
                parts[r, slot] = jnp.where(low_lanes, first, second)
            return carry

        lax.fori_loop(0, size, body, 0)
        span = pl.ds(base, size)
        return [
            remote(
                parts.at[peer, span], arrived.at[d, span],
                part_send.at[g, d], part_recv.at[g, d], (peer, my_col),
            )
            for d, peer in enumerate(row_peers)
        ]

    def start_solved(g, copies):
        h, base, size = plan.groups[g]
        for copy in copies:
            copy.wait_recv()

        def body(n, carry):
            slot = base + n
            total = parts[my_row, slot]
            for d in range(rows - 1):
                total = total + arrived[d, slot]
            total = jnp.where(row_ids < live[slot], total, 0.0)
            solved[my_row, slot] = total
            flip[:half] = total
            flip[half:] = pltpu.roll(total, 64, 1)
            even, odd = flip[pl.ds(0, half, stride=2)], flip[pl.ds(1, half, stride=2)]
            out[slot] = jnp.where(low_lanes, even, pltpu.roll(odd, 64, 1))
            return carry

        lax.fori_loop(0, size, body, 0)
        if h == LEVELS - 1:
            return []
        span = pl.ds(base, size)
        return [
            remote(
                solved.at[my_row, span], solved.at[my_row, span],
                sol_send.at[g, d], sol_recv.at[g, d], (peer, my_col),
            )
            for d, peer in enumerate(row_peers)
        ]

    def widen(g, copies):
        h, base, size = plan.groups[g]
        for copy in copies:
            copy.wait_recv()

        def body(n, carry):
            for r in range(rows):
                wide[n, pl.ds(r * piece, piece)] = split_pair(solved[r, base + n], low_lanes)
            return carry

        lax.fori_loop(0, size, body, 0)
        for slot in range(base, base + size):
            panel_loads[slot].wait()

    def contribute(g, first, last):
        h, base, size = plan.groups[g]
        if first >= last:
            return

        def body(n, carry):
            place = lax.rem(base + n, RING)
            pair = wide[n]
            for a in range(first, last):
                high, low = two_part(ring[place, a])
                both = jnp.dot(high, pair, preferred_element_type=jnp.float32)
                both += jnp.dot(low, pair, preferred_element_type=jnp.float32)
                both += pltpu.roll(both, 64, 1)
                blocks[n, a] = jnp.where(low_lanes, both[:half], both[half:])
            return carry

        lax.fori_loop(0, size, body, 0)
        for a in range(first, last):
            up = h + 1 + a
            goals = [target[(base + n) * 7 + a] for n in range(size)]
            scales = [weight[(base + n) * 7 + a] for n in range(size)]

            def scatter(t, carry, a=a, up=up, goals=goals, scales=scales):
                total = pend[plan.pend_base[up] + t]
                for n in range(size):
                    total = total + jnp.where(goals[n] == t, scales[n], 0.0) * blocks[n, a]
                pend[plan.pend_base[up] + t] = total
                return carry

            lax.fori_loop(0, plan.slots[up] * cols, scatter, 0)

    def start_near(h):
        count = plan.slots[h] * depth
        return remote(
            pend.at[pl.ds(plan.pend_base[h] + (1 - my_core) * count, count)],
            near.at[pl.ds(plan.half_base[h], count)],
            near_sem.at[0, h], near_sem.at[1, h], (my_row, mate),
        )

    def start_far(h, copy):
        count = plan.slots[h] * depth
        mine = plan.pend_base[h] + my_core * count
        copy.wait_recv()

        for g in group_ids[h]:
            _, base, size = plan.groups[g]
            start = base - plan.slot_base[h]

            def body(i, carry, start=start, size=size):
                spot = lax.div(i, size) * plan.slots[h] + start + lax.rem(i, size)
                pend[mine + spot] = pend[mine + spot] + near[plan.half_base[h] + spot]
                return carry

            lax.fori_loop(0, depth * size, body, 0)
            arriving[g] = [
                remote(
                    pend.at[pl.ds(mine + z * plan.slots[h] + start, size)],
                    far.at[pl.ds(plan.far_base[h] + d * plan.slots[h] + start, size)],
                    far_send.at[g, d], far_recv.at[g, d], (my_row, z * 2 + my_core),
                )
                for d, z in enumerate(z_peers)
            ]

    group_ids = {h: [g for g, one in enumerate(plan.groups) if one[0] == h] for h in range(LEVELS)}
    arriving = {}

    def finish(g):
        h, base, size = plan.groups[g]
        reach = LEVELS - 1 - h
        if reach == 0:
            return
        final = g == group_ids[h][-1]
        widen(g, sharing[g])
        contribute(g, 0, 1)
        if final:
            near_copy = start_near(h + 1)
        contribute(g, 1, min(2, reach))
        if final:
            start_far(h + 1, near_copy)
        contribute(g, 2, reach)
        for slot in range(base, base + size):
            load_panel(slot + RING)

    waiting, sharing = {}, {}
    for h in range(LEVELS):
        ids = group_ids[h]
        loads[h].wait()
        if h == 0:
            waiting.update({g: start_partial(g) for g in ids})
        for i in range(len(ids) + 2):
            if i < len(ids) and h > 0:
                for copy in arriving[ids[i]]:
                    copy.wait_recv()
                waiting[ids[i]] = start_partial(ids[i])
            if 0 <= i - 1 < len(ids):
                sharing[ids[i - 1]] = start_solved(ids[i - 1], waiting[ids[i - 1]])
            if i >= 2:
                finish(ids[i - 2])
    for copy in sends:
        copy.wait_send()


def on_device(right_side, inverse_rows, panels, pattern, node_sizes, parent):
    rows, cols = lax.axis_size("prow"), lax.axis_size("pcol")
    plan = Plan(rows, cols)
    slots, piece, full = plan.total, panels.shape[3], panels.shape[4]
    count = right_side.shape[2] // piece
    half = piece // 2
    packed = right_side.reshape(slots, half, 2 * count)
    groups = len(plan.groups)
    dma = pltpu.SemaphoreType.DMA
    vmem = pl.BlockSpec(memory_space=pltpu.VMEM)
    smem = pl.BlockSpec(memory_space=pltpu.SMEM)
    anywhere = pl.BlockSpec(memory_space=pl.ANY)
    block = (half, 2 * count)
    solved = pl.pallas_call(
        functools.partial(kernel, plan),
        out_shape=jax.ShapeDtypeStruct((slots,) + block, jnp.float32),
        in_specs=[smem, smem, smem, vmem, anywhere, anywhere],
        out_specs=vmem,
        scratch_shapes=[
            pltpu.VMEM((slots, piece, full), jnp.float32),
            pltpu.VMEM((RING, LEVELS - 1, piece, full), jnp.float32),
            pltpu.VMEM((plan.pend,) + block, jnp.float32),
            pltpu.VMEM((plan.half,) + block, jnp.float32),
            pltpu.VMEM((plan.far,) + block, jnp.float32),
            pltpu.VMEM((rows, slots) + block, jnp.float32),
            pltpu.VMEM((rows - 1, slots) + block, jnp.float32),
            pltpu.VMEM((rows, slots) + block, jnp.float32),
            pltpu.VMEM((GROUP, full, 2 * count), jnp.bfloat16),
            pltpu.VMEM((GROUP, LEVELS - 1) + block, jnp.float32),
            pltpu.SMEM((slots * 7,), jnp.int32),
            pltpu.SMEM((slots * 7,), jnp.float32),
            pltpu.SMEM((slots,), jnp.int32),
            pltpu.VMEM((piece, 2 * count), jnp.float32),
            dma((LEVELS,)),
            dma((RING,)),
            dma((2, LEVELS)),
            dma((groups, plan.depth - 1)),
            dma((groups, plan.depth - 1)),
            dma((groups, rows - 1)),
            dma((groups, rows - 1)),
            dma((groups, rows - 1)),
            dma((groups, rows - 1)),
        ],
        compiler_params=pltpu.CompilerParams(
            collective_id=0, has_side_effects=True, vmem_limit_bytes=60 * 1024 * 1024
        ),
    )(
        parent,
        pattern,
        node_sizes,
        packed,
        inverse_rows.reshape(slots, piece, full),
        panels.reshape(slots, LEVELS - 1, piece, full),
    )
    return solved.reshape(slots, 1, piece * count)


def solution(mesh):
    in_specs = (
        P(None, "pcol", "prow"),
        P(None, "pcol", "prow", None),
        P(None, "pcol", None, "prow", None),
        P(None, "pcol", None),
        P(None, "pcol"),
        P(),
    )
    out_specs = P(None, "pcol", "prow")
    return jax.shard_map(
        on_device, mesh=mesh, in_specs=in_specs, out_specs=out_specs, check_vma=False
    )
```

```python
import functools

import jax
import jax.numpy as jnp
from jax import lax
from jax.experimental import pallas as pl
from jax.experimental.pallas import tpu as pltpu
from jax.sharding import PartitionSpec as P

LEVELS = 8
LEAVES = 128
GROUP = 4
RING = 12
WIDE = 16
MESH = pl.DeviceIdType.MESH


class Plan:
    def __init__(self, rows, cols):
        self.rows, self.cols = rows, cols
        self.depth = cols // 2
        self.nodes = [LEAVES >> h for h in range(LEVELS)]
        self.slots = [max(1, n // cols) for n in self.nodes]
        self.slot_base, self.node_base, self.pend_base = [], [], []
        self.half_base, self.far_base = [], []
        s = n = p = c = f = 0
        for h in range(LEVELS):
            self.slot_base.append(s)
            self.node_base.append(n)
            self.pend_base.append(p)
            self.half_base.append(c)
            self.far_base.append(f)
            s += self.slots[h]
            n += self.nodes[h]
            if h > 0:
                p += self.slots[h] * cols
                c += self.slots[h] * self.depth
                f += self.slots[h] * (self.depth - 1)
        self.total, self.pend, self.half, self.far = s, p, c, f
        self.groups = []
        for h in range(LEVELS):
            size = GROUP if h == 0 else min(2, max(1, self.slots[h] // 2))
            size = min(size, self.slots[h])
            for start in range(0, self.slots[h], size):
                self.groups.append((h, self.slot_base[h] + start, size))
        self.level_of = [h for h in range(LEVELS) for _ in range(self.slots[h])]


def split_pair(packed, low_lanes):
    high = packed.astype(jnp.bfloat16).astype(jnp.float32)
    low = packed - high
    top = jnp.where(low_lanes, high, pltpu.roll(low, 64, 1))
    bottom = jnp.where(low_lanes, pltpu.roll(high, 64, 1), low)
    return jnp.concatenate([top, bottom], 0).astype(jnp.bfloat16)


def two_part(matrix):
    high = matrix.astype(jnp.bfloat16)
    low = (matrix - high.astype(jnp.float32)).astype(jnp.bfloat16)
    return high, low


def kernel(
    plan, parent, pattern, sizes, rhs, inverse_hbm, panels_hbm, out,
    inverse, ring, pend, near, far, parts, arrived, solved, wide, blocks,
    target, weight, live, flip,
    inverse_sem, ring_sem, near_sem, far_send, far_recv, part_send, part_recv, sol_send, sol_recv,
):
    rows, cols, depth = plan.rows, plan.cols, plan.depth
    piece = inverse.shape[1]
    half = piece // 2
    my_row, my_col = lax.axis_index("prow"), lax.axis_index("pcol")
    my_core, my_z = lax.rem(my_col, 2), lax.div(my_col, 2)
    row_peers = [lax.rem(my_row + d, rows) for d in range(1, rows)]
    z_peers = [lax.rem(my_z + d, depth) for d in range(1, depth)]
    mate = my_col + 1 - 2 * my_core

    loads = []
    for h in range(LEVELS):
        span = pl.ds(plan.slot_base[h], plan.slots[h])
        copy = pltpu.make_async_copy(inverse_hbm.at[span], inverse.at[span], inverse_sem.at[h])
        copy.start()
        loads.append(copy)
    panel_loads = {}

    def load_panel(slot):
        if slot >= plan.total:
            return
        reach = LEVELS - 1 - plan.level_of[slot]
        if reach == 0:
            return
        place = slot % RING
        copy = pltpu.make_async_copy(
            panels_hbm.at[slot, pl.ds(0, reach)], ring.at[place, pl.ds(0, reach)], ring_sem.at[place]
        )
        copy.start()
        panel_loads[slot] = copy

    for slot in range(min(RING, plan.total)):
        load_panel(slot)

    barrier = pltpu.get_barrier_semaphore()
    greeted = [(p, my_col) for p in row_peers] + [(my_row, mate)]
    greeted += [(my_row, z * 2 + my_core) for z in z_peers]
    for who in greeted:
        pl.semaphore_signal(barrier, inc=1, device_id=who, device_id_type=MESH)

    for h in range(LEVELS):

        def measure_live(i, carry, h=h):
            slot = plan.slot_base[h] + i
            live[slot] = jnp.where(i * cols + my_col < plan.nodes[h], sizes[slot, 0], 0)
            return carry

        lax.fori_loop(0, plan.slots[h], measure_live, 0)

    def describe_targets():
        for h in range(LEVELS):

            def describe(i, carry, h=h):
                slot = plan.slot_base[h] + i
                place = i * cols + my_col
                real = place < plan.nodes[h]
                node = plan.node_base[h] + jnp.minimum(place, plan.nodes[h] - 1)
                for a in range(LEVELS - 1 - h):
                    up = h + 1 + a
                    node = parent[node]
                    local = node - plan.node_base[up]
                    owner = lax.rem(local, cols)
                    spot = lax.rem(owner, 2) * depth + lax.div(owner, 2)
                    target[slot * 7 + a] = spot * plan.slots[up] + lax.div(local, cols)
                    weight[slot * 7 + a] = jnp.where(real, pattern[slot, 0, a], 0).astype(jnp.float32)
                return carry

            lax.fori_loop(0, plan.slots[h], describe, 0)

        def clear(i, carry):
            pend[i] = jnp.zeros_like(pend[i])
            return carry

        lax.fori_loop(0, plan.pend, clear, 0)
        lax.fori_loop(plan.slots[0], plan.total, pack_halves, 0)

    lane = lax.broadcasted_iota(jnp.int32, (half, 128), 1)
    low_lanes = lane < 64
    row_ids = (
        my_row * piece
        + lax.broadcasted_iota(jnp.int32, (half, 128), 0)
        + jnp.where(low_lanes, 0, half)
    )
    contract_first = (((0,), (0,)), ((), ()))
    sends = []

    def pack_halves(slot, carry):
        pairs = rhs[slot]
        flip[pl.ds(0, half, stride=2)] = pairs
        flip[pl.ds(1, half, stride=2)] = pltpu.roll(pairs, 64, 1)
        out[slot] = jnp.where(low_lanes, flip[:half], pltpu.roll(flip[half:], 64, 1))
        return carry

    lax.fori_loop(0, plan.slots[0], pack_halves, 0)

    pl.semaphore_wait(barrier, len(greeted))

    def remote(src, dst, send_sem, recv_sem, who):
        copy = pltpu.make_async_remote_copy(
            src_ref=src, dst_ref=dst, send_sem=send_sem, recv_sem=recv_sem,
            device_id=who, device_id_type=MESH,
        )
        copy.start()
        sends.append(copy)
        return copy

    def start_partial(g):
        h, base, size = plan.groups[g]

        def body(n, carry):
            slot = base + n
            residue = out[slot]
            if h > 0:
                step = slot - plan.slot_base[h]
                own = (my_core * depth + my_z) * plan.slots[h] + step
                update = pend[plan.pend_base[h] + own]
                for d in range(depth - 1):
                    update = update + far[plan.far_base[h] + d * plan.slots[h] + step]
                residue = residue - update
            scaled = jnp.where(row_ids < live[slot], residue, 0.0)
            pair = split_pair(scaled, low_lanes)
            high, low = two_part(inverse[slot])
            both = lax.dot_general(high, pair, contract_first, preferred_element_type=jnp.float32)
            both += lax.dot_general(low, pair, contract_first, preferred_element_type=jnp.float32)
            both += pltpu.roll(both, 64, 1)
            for r in range(rows):
                first = both[r * piece : r * piece + half]
                second = both[r * piece + half : (r + 1) * piece]
                parts[r, slot] = jnp.where(low_lanes, first, second)
            return carry

        lax.fori_loop(0, size, body, 0)
        span = pl.ds(base, size)
        return [
            remote(
                parts.at[peer, span], arrived.at[d, span],
                part_send.at[g, d], part_recv.at[g, d], (peer, my_col),
            )
            for d, peer in enumerate(row_peers)
        ]

    def start_solved(g, copies):
        h, base, size = plan.groups[g]
        for copy in copies:
            copy.wait_recv()

        def body(n, carry):
            slot = base + n
            total = parts[my_row, slot]
            for d in range(rows - 1):
                total = total + arrived[d, slot]
            total = jnp.where(row_ids < live[slot], total, 0.0)
            solved[my_row, slot] = total
            flip[:half] = total
            flip[half:] = pltpu.roll(total, 64, 1)
            even, odd = flip[pl.ds(0, half, stride=2)], flip[pl.ds(1, half, stride=2)]
            out[slot] = jnp.where(low_lanes, even, pltpu.roll(odd, 64, 1))
            return carry

        lax.fori_loop(0, size, body, 0)
        if h == LEVELS - 1:
            return []
        span = pl.ds(base, size)
        return [
            remote(
                solved.at[my_row, span], solved.at[my_row, span],
                sol_send.at[g, d], sol_recv.at[g, d], (peer, my_col),
            )
            for d, peer in enumerate(row_peers)
        ]

    def widen(g, copies):
        h, base, size = plan.groups[g]
        for copy in copies:
            copy.wait_recv()

        def body(n, carry):
            for r in range(rows):
                wide[lax.rem(base + n, WIDE), pl.ds(r * piece, piece)] = split_pair(solved[r, base + n], low_lanes)
            return carry

        lax.fori_loop(0, size, body, 0)
        for slot in range(base, base + size):
            panel_loads[slot].wait()

    def contribute(g, first, last):
        h, base, size = plan.groups[g]
        if first >= last:
            return

        def body(n, carry):
            place = lax.rem(base + n, RING)
            pair = wide[lax.rem(base + n, WIDE)]
            for a in range(first, last):
                high, low = two_part(ring[place, a])
                both = jnp.dot(high, pair, preferred_element_type=jnp.float32)
                both += jnp.dot(low, pair, preferred_element_type=jnp.float32)
                both += pltpu.roll(both, 64, 1)
                blocks[n, a] = jnp.where(low_lanes, both[:half], both[half:])
            return carry

        lax.fori_loop(0, size, body, 0)
        for a in range(first, last):
            up = h + 1 + a
            goals = [target[(base + n) * 7 + a] for n in range(size)]
            scales = [weight[(base + n) * 7 + a] for n in range(size)]

            def scatter(t, carry, a=a, up=up, goals=goals, scales=scales):
                total = pend[plan.pend_base[up] + t]
                for n in range(size):
                    total = total + jnp.where(goals[n] == t, scales[n], 0.0) * blocks[n, a]
                pend[plan.pend_base[up] + t] = total
                return carry

            lax.fori_loop(0, plan.slots[up] * cols, scatter, 0)

    def start_near(h):
        count = plan.slots[h] * depth
        return remote(
            pend.at[pl.ds(plan.pend_base[h] + (1 - my_core) * count, count)],
            near.at[pl.ds(plan.half_base[h], count)],
            near_sem.at[0, h], near_sem.at[1, h], (my_row, mate),
        )

    def start_far(h, copy):
        count = plan.slots[h] * depth
        mine = plan.pend_base[h] + my_core * count
        copy.wait_recv()

        for g in group_ids[h]:
            _, base, size = plan.groups[g]
            start = base - plan.slot_base[h]

            def body(i, carry, start=start, size=size):
                spot = lax.div(i, size) * plan.slots[h] + start + lax.rem(i, size)
                pend[mine + spot] = pend[mine + spot] + near[plan.half_base[h] + spot]
                return carry

            lax.fori_loop(0, depth * size, body, 0)
            arriving[g] = [
                remote(
                    pend.at[pl.ds(mine + z * plan.slots[h] + start, size)],
                    far.at[pl.ds(plan.far_base[h] + d * plan.slots[h] + start, size)],
                    far_send.at[g, d], far_recv.at[g, d], (my_row, z * 2 + my_core),
                )
                for d, z in enumerate(z_peers)
            ]

    group_ids = {h: [g for g, one in enumerate(plan.groups) if one[0] == h] for h in range(LEVELS)}
    arriving = {}

    def finish(g):
        h, base, size = plan.groups[g]
        reach = LEVELS - 1 - h
        if reach == 0:
            return
        final = g == group_ids[h][-1]
        widen(g, sharing[g])
        contribute(g, 0, 1)
        if final:
            near_copy = start_near(h + 1)
        if final or h > 0 or g == 0:
            contribute(g, 1, min(2, reach))
        if final:
            start_far(h + 1, near_copy)
        if h == 0 and g > 0:
            later.append((g, 2 if final else 1))
        else:
            contribute(g, 2, reach)
            release(g)

    def release(g):
        _, base, size = plan.groups[g]
        for slot in range(base, base + size):
            load_panel(slot + RING)

    def catch_up():
        if later:
            g, first = later.pop(0)
            contribute(g, first, LEVELS - 1)
            release(g)

    later = []
    waiting, sharing = {}, {}
    for h in range(LEVELS):
        ids = group_ids[h]
        loads[h].wait()
        if h == 0:
            waiting.update({g: start_partial(g) for g in ids})
            describe_targets()
        if h == 1:
            catch_up()
        for i in range(len(ids) + 2):
            if i < len(ids) and h > 0:
                for copy in arriving[ids[i]]:
                    copy.wait_recv()
                waiting[ids[i]] = start_partial(ids[i])
            if 0 <= i - 1 < len(ids):
                sharing[ids[i - 1]] = start_solved(ids[i - 1], waiting[ids[i - 1]])
            if h > 0:
                catch_up()
            if i >= 2:
                while later and h > 0:
                    catch_up()
                finish(ids[i - 2])
    for copy in sends:
        copy.wait_send()


def on_device(right_side, inverse_rows, panels, pattern, node_sizes, parent):
    rows, cols = lax.axis_size("prow"), lax.axis_size("pcol")
    plan = Plan(rows, cols)
    slots, piece, full = plan.total, panels.shape[3], panels.shape[4]
    count = right_side.shape[2] // piece
    half = piece // 2
    packed = right_side.reshape(slots, half, 2 * count)
    groups = len(plan.groups)
    dma = pltpu.SemaphoreType.DMA
    vmem = pl.BlockSpec(memory_space=pltpu.VMEM)
    smem = pl.BlockSpec(memory_space=pltpu.SMEM)
    anywhere = pl.BlockSpec(memory_space=pl.ANY)
    block = (half, 2 * count)
    solved = pl.pallas_call(
        functools.partial(kernel, plan),
        out_shape=jax.ShapeDtypeStruct((slots,) + block, jnp.float32),
        in_specs=[smem, smem, smem, vmem, anywhere, anywhere],
        out_specs=vmem,
        scratch_shapes=[
            pltpu.VMEM((slots, piece, full), jnp.float32),
            pltpu.VMEM((RING, LEVELS - 1, piece, full), jnp.float32),
            pltpu.VMEM((plan.pend,) + block, jnp.float32),
            pltpu.VMEM((plan.half,) + block, jnp.float32),
            pltpu.VMEM((plan.far,) + block, jnp.float32),
            pltpu.VMEM((rows, slots) + block, jnp.float32),
            pltpu.VMEM((rows - 1, slots) + block, jnp.float32),
            pltpu.VMEM((rows, slots) + block, jnp.float32),
            pltpu.VMEM((WIDE, full, 2 * count), jnp.bfloat16),
            pltpu.VMEM((GROUP, LEVELS - 1) + block, jnp.float32),
            pltpu.SMEM((slots * 7,), jnp.int32),
            pltpu.SMEM((slots * 7,), jnp.float32),
            pltpu.SMEM((slots,), jnp.int32),
            pltpu.VMEM((piece, 2 * count), jnp.float32),
            dma((LEVELS,)),
            dma((RING,)),
            dma((2, LEVELS)),
            dma((groups, plan.depth - 1)),
            dma((groups, plan.depth - 1)),
            dma((groups, rows - 1)),
            dma((groups, rows - 1)),
            dma((groups, rows - 1)),
            dma((groups, rows - 1)),
        ],
        compiler_params=pltpu.CompilerParams(
            collective_id=0, has_side_effects=True, vmem_limit_bytes=60 * 1024 * 1024
        ),
    )(
        parent,
        pattern,
        node_sizes,
        packed,
        inverse_rows.reshape(slots, piece, full),
        panels.reshape(slots, LEVELS - 1, piece, full),
    )
    return solved.reshape(slots, 1, piece * count)


def solution(mesh):
    in_specs = (
        P(None, "pcol", "prow"),
        P(None, "pcol", "prow", None),
        P(None, "pcol", None, "prow", None),
        P(None, "pcol", None),
        P(None, "pcol"),
        P(),
    )
    out_specs = P(None, "pcol", "prow")
    return jax.shard_map(
        on_device, mesh=mesh, in_specs=in_specs, out_specs=out_specs, check_vma=False
    )
```
